32 devices in a mesh: dp: 16 (over z, y, x), proto: 2 (over core).
Axes of the slice: x: 2, y: 2, z: 4, core: 2. Of those that a mesh axis runs over, the one named last changes fastest.
Arguments:
- teacher_feats: bfloat16 [8192, 256], P('dp'), may hold values from -0.5 to 0.5
- student_feats: bfloat16 [8192, 256], P('dp'), may hold values from -0.5 to 0.5
- teacher_protos: bfloat16 [32768, 256], P('proto'), may hold values from -0.5 to 0.5
- student_protos: bfloat16 [32768, 256], P('proto'), may hold values from -0.5 to 0.5
Outputs:
- proto_grad: float32 [32768, 256], P(('proto', 'dp'))
- feature_grad: float32 [8192, 256], P('dp')
The draws below stay inside these ranges and needn't reach their ends.
All inputs are finite; a program needn't handle non-finite values.
Results may differ from the reference program's by a relative error of at most 0.0022.
Values may be sent and summed in bfloat16 or wider, within the bound.
A program may use at most 256 MiB of HBM per device.

```python
import math
import jax
import jax.numpy as jnp
from jax import lax

BOT = 256
PROTOS = 32768
ITERS = 3
IMAGES = 8192


def shared_dir(key):
    bits = jax.random.randint(jax.random.fold_in(key, 97), (BOT,), 0, 2)
    return (2 * bits - 1).astype(jnp.float32) * BOT ** (-0.5)


def proto_rows(key, direction, top):
    keys = jax.random.split(key, 1)
    mix = (jnp.arange(PROTOS, dtype=jnp.float32) + 0.5) * (top / PROTOS)
    noise = jax.random.normal(keys[0], (PROTOS, BOT), jnp.float32) * 0.0625
    value = mix[:, None] * direction[None, :] + jnp.sqrt(1.0 - mix * mix)[:, None] * noise
    return jnp.clip(value, -0.5, 0.5).astype(jnp.bfloat16)


def draw_teacher_protos(key, part):
    direction = shared_dir(key)
    key = jax.random.fold_in(key, 21)
    return proto_rows(key, direction, 0.5)


def draw_student_protos(key, part):
    direction = shared_dir(key)
    key = jax.random.fold_in(key, 31)
    return proto_rows(key, direction, 0.5)


def draw_student_feats(key, part):
    direction = shared_dir(key)
    key = jax.random.fold_in(key, 41)
    keys = jax.random.split(key, 2)
    along = jax.random.uniform(keys[0], (IMAGES, 1), jnp.float32, -0.8, 0.8)
    noise = jax.random.normal(keys[1], (IMAGES, BOT), jnp.float32) * 0.0625
    value = along * direction[None, :] + noise
    return jnp.clip(value, -0.5, 0.5).astype(jnp.bfloat16)


def draw_teacher_feats(key, part):
    direction = shared_dir(key)
    key = jax.random.fold_in(key, 11)
    keys = jax.random.split(key, 5)
    centers = jax.random.normal(keys[0], (8, BOT), jnp.float32) * 0.0625
    members = jax.random.randint(keys[1], (IMAGES,), 0, 8)
    ramp = ((jnp.arange(IMAGES, dtype=jnp.float32) + 0.5) * (2.0 / IMAGES) - 1.0)[:, None]
    strength = jax.random.uniform(keys[2], (IMAGES, 1), jnp.float32, 0.5, 2.0)
    noise = jax.random.normal(keys[3], (IMAGES, BOT), jnp.float32) * 0.0625
    along = ramp + jax.random.uniform(keys[4], (IMAGES, 1), jnp.float32, -0.2, 0.2)
    value = strength * centers[members] + along * direction[None, :] + noise
    return jnp.clip(value, -0.5, 0.5).astype(jnp.bfloat16)


def setup_inputs(seed: int = 0) -> dict:
    seeds = jax.random.split(jax.random.key(seed), 5)
    return {
        "teacher_feats": draw_teacher_feats(jax.random.fold_in(seeds[4], 71), 0),
        "student_feats": draw_student_feats(jax.random.fold_in(seeds[4], 71), 0),
        "teacher_protos": draw_teacher_protos(jax.random.fold_in(seeds[4], 71), 0),
        "student_protos": draw_student_protos(jax.random.fold_in(seeds[4], 71), 0),
    }


teacher_temp = 0.07
student_temp = 0.1
norm_eps = 1e-06

def unit_rows(value):
    wide = value.astype(jnp.float32)
    factor = lax.rsqrt(lax.optimization_barrier(jnp.sum(wide * wide, axis=-1, keepdims=True)) + norm_eps)
    return (wide * factor, factor, wide)

def scores(left, right, temp):
    prod = lax.dot_general(left, right, (((1,), (1,)), ((), ())), preferred_element_type=jnp.float32)
    return jnp.exp(prod / temp)

def reference(teacher_feats, student_feats, teacher_protos, student_protos):
    t_unit, _, _ = unit_rows(teacher_feats)
    t_dir = t_unit.astype(jnp.bfloat16)
    s_unit, s_fac, s_wide = unit_rows(student_feats)
    s_dir = s_unit.astype(jnp.bfloat16)
    tw_unit, _, _ = unit_rows(teacher_protos)
    t_w = tw_unit.astype(jnp.bfloat16)
    sw_unit, sw_fac, sw_wide = unit_rows(student_protos)
    s_w = sw_unit.astype(jnp.bfloat16)
    block = min(512, IMAGES)
    count = IMAGES // block
    t_blocks = t_dir.reshape(count, block, BOT)
    s_blocks = s_dir.reshape(count, block, BOT)

    def first_pass(total, rows):
        return (total + lax.optimization_barrier(jnp.sum(scores(rows, t_w, teacher_temp), axis=0)), None)
    col, _ = lax.scan(first_pass, jnp.zeros((PROTOS,), jnp.float32), t_blocks)
    proto_scale = 1.0 / col
    for step in range(ITERS - 1):

        def mid_pass(total, rows, scale=proto_scale):
            expo = scores(rows, t_w, teacher_temp)
            row_scale = 1.0 / lax.optimization_barrier(jnp.sum(expo * scale, axis=1))
            return (total + lax.optimization_barrier(jnp.sum(expo * row_scale[:, None], axis=0)), None)
        col, _ = lax.scan(mid_pass, jnp.zeros((PROTOS,), jnp.float32), t_blocks)
        proto_scale = 1.0 / col

    def last_pass(total, pair):
        t_rows, s_rows = pair
        weighted = scores(t_rows, t_w, teacher_temp) * proto_scale
        targets = weighted * (1.0 / lax.optimization_barrier(jnp.sum(weighted, axis=1)))[:, None]
        expo_s = scores(s_rows, s_w, student_temp)
        probs = expo_s * (1.0 / lax.optimization_barrier(jnp.sum(expo_s, axis=1)))[:, None]
        diff = (probs - targets).astype(jnp.bfloat16)
        total = total + lax.dot_general(diff, s_rows, (((0,), (0,)), ((), ())), preferred_element_type=jnp.float32)
        feat = jnp.dot(diff, s_w, preferred_element_type=jnp.float32)
        return (total, feat)
    summed, feats = lax.scan(last_pass, jnp.zeros((PROTOS, BOT), jnp.float32), (t_blocks, s_blocks))
    gw = summed * (PROTOS / (student_temp * math.sqrt(IMAGES)))
    proto_grad = sw_fac * gw - sw_wide * (sw_fac * sw_fac * sw_fac) * lax.optimization_barrier(jnp.sum(sw_wide * gw, axis=-1, keepdims=True))
    gz = feats.reshape(IMAGES, BOT) * (math.sqrt(PROTOS) / student_temp)
    feature_grad = s_fac * gz - s_wide * (s_fac * s_fac * s_fac) * lax.optimization_barrier(jnp.sum(s_wide * gz, axis=-1, keepdims=True))
    return (proto_grad, feature_grad)
```

```python
import functools
import math

import jax
import jax.numpy as jnp
from jax import lax
from jax.experimental import pallas as pl
from jax.experimental.pallas import tpu as pltpu
from jax.sharding import PartitionSpec as P

ITERS = 3
OUTER = 4

teacher_temp = 0.07
student_temp = 0.1
norm_eps = 1e-06
LOG2E = math.log2(math.e)
MESH = pl.DeviceIdType.MESH
f32 = jnp.float32
bf16 = jnp.bfloat16


def dot(a, b, dims):
    return lax.dot_general(a, b, ((dims[:1], dims[1:]), ((), ())), preferred_element_type=f32)


def factor_of(wide):
    return lax.rsqrt(jnp.sum(wide * wide, axis=-1, keepdims=True) + norm_eps)


def unit(value):
    wide = value.astype(f32)
    return (wide * factor_of(wide)).astype(bf16)


def kernel(
    inner, cores, protos_all, images_all,
    tf, sf, tp, sp, out_p, out_f,
    expo, tw, sw, vown, tdir, sdir, sdir_t, rscale, tscale, cacc, tacc, diffs,
    gws, gwr, feat, fxs, fxr, fzs, fzr, fo, colb, psb, rowb,
    lsem, g1s, g1r, g2s, g2r, cs, cr, rs, rr, ws, wr, xs, xr, zs, zr, os_, or_,
):
    block = tf.shape[0]
    strip = block // cores
    images, protos = expo.shape
    rows_out = out_p.shape[0]
    width = min(512, protos)
    chunks = protos // width
    group = OUTER * cores
    d, c = lax.axis_index("dp"), lax.axis_index("proto")
    o, q = d // inner, lax.rem(d, inner)
    g = o * cores + c
    kt, ks = LOG2E / teacher_temp, LOG2E / student_temp

    def col_peer(k):
        return (o * inner + lax.rem(q + k, inner), c)

    def row_peer(k):
        h = lax.rem(g + k, group)
        return ((h // cores) * inner + q, lax.rem(h, cores))

    def z_peer(k):
        return (lax.rem(o + k, OUTER) * inner + q, c)

    def core_peer(j):
        return (d, lax.rem(c + j, cores))

    def from_z(k):
        return lax.rem(o + OUTER - k, OUTER)

    def from_core(j):
        return lax.rem(c + cores - j, cores)

    def aligned(start, size):
        return pl.ds(pl.multiple_of(start, size), size)

    def remote(src, dst, ss, rsm, dev):
        return pltpu.make_async_remote_copy(
            src_ref=src, dst_ref=dst, send_sem=ss, recv_sem=rsm,
            device_id=dev, device_id_type=MESH,
        )

    load_t = pltpu.make_async_copy(tp.at[aligned(o * protos, protos)], tw, lsem.at[0])
    load_s = pltpu.make_async_copy(sp.at[aligned(o * protos, protos)], sw, lsem.at[1])
    load_v = pltpu.make_async_copy(sp.at[aligned(d * rows_out, rows_out)], vown, lsem.at[2])
    load_t.start()
    load_s.start()
    load_v.start()

    barrier = pltpu.get_barrier_semaphore()
    for k in range(1, inner):
        pl.semaphore_signal(barrier, inc=1, device_id=col_peer(k), device_id_type=MESH)
    for k in range(1, group):
        pl.semaphore_signal(barrier, inc=1, device_id=row_peer(k), device_id_type=MESH)
    own = aligned(o * block, block)
    tdir[own, :] = unit(tf[...])
    sdir[own, :] = unit(sf[...])
    pl.semaphore_wait(barrier, inner - 1 + group - 1)

    pending = []

    def strip_rows(buf, ob, part):
        return buf.at[aligned(ob * block + part * strip, strip)]

    def gather_first(n, buf):
        for k in range(1, OUTER):
            part = strip_rows(buf, o, c)
            copy = remote(part, part, g1s.at[n, k], g1r.at[n, k], z_peer(k))
            copy.start()
            pending.append(copy)

    def gather_forward(n, buf):
        for k in range(1, OUTER):
            part = strip_rows(buf, from_z(k), c)
            remote(part, part, g1s.at[n, k], g1r.at[n, k], z_peer(k)).wait_recv()
            for j in range(1, cores):
                copy = remote(part, part, g2s.at[n, k, j], g2r.at[n, k, j], core_peer(j))
                copy.start()
                pending.append(copy)

    def gather_wait(n, buf, k):
        for j in range(1, cores):
            part = strip_rows(buf, from_z(k), from_core(j))
            remote(part, part, g2s.at[n, k, j], g2r.at[n, k, j], core_peer(j)).wait_recv()

    gather_first(0, tdir)
    gather_first(1, sdir)

    def normalize(buf):
        def body(n, _):
            rows = aligned(n * width, width)
            buf[rows, :] = unit(buf[rows, :])
            return 0
        lax.fori_loop(0, chunks, body, 0)

    load_t.wait()
    normalize(tw)

    cacc[...] = jnp.zeros_like(cacc)

    def teacher_block(ob):
        rows = aligned(ob * block, block)

        def body(n, _):
            cols = aligned(n * width, width)
            e = jnp.exp2(dot(tdir[rows, :], tw[cols, :], (1, 1)) * kt)
            expo[rows, cols] = e
            cacc[:, cols] += jnp.sum(e.reshape(block // 8, 8, width), axis=0)
            return 0
        lax.fori_loop(0, chunks, body, 0)

    def student_block(ob):
        rows = aligned(ob * block, block)
        tacc[...] = jnp.zeros_like(tacc)

        def body(n, _):
            cols = aligned(n * width, width)
            e = jnp.exp2(dot(sdir[rows, :], sw[cols, :], (1, 1)) * ks)
            part = e[:, :128]
            for i in range(1, width // 128):
                part += e[:, i * 128:(i + 1) * 128]
            tacc[...] += part
            return 0
        lax.fori_loop(0, chunks, body, 0)
        for i in range(block // 128):
            line = jnp.sum(tacc[i * 128:(i + 1) * 128, :].T, axis=0, keepdims=True)
            rowb[ITERS, 0, pl.ds(ob * (block // 128) + i, 1), :] = line
        sdir_t[:, rows] = sdir[rows, :].T

    def send_cols(it):
        colb[it, 0] = jnp.sum(cacc[...], axis=0, keepdims=True)
        for k in range(1, inner):
            copy = remote(colb.at[it, 0], colb.at[it, k], cs.at[it, k], cr.at[it, k], col_peer(k))
            copy.start()
            pending.append(copy)

    def take_cols(it):
        total = colb[it, 0]
        for k in range(1, inner):
            remote(colb.at[it, 0], colb.at[it, k], cs.at[it, k], cr.at[it, k], col_peer(k)).wait_recv()
            total = total + colb[it, k]
        psb[...] = 1.0 / total

    def send_rows(it):
        for k in range(1, group):
            copy = remote(rowb.at[it, 0], rowb.at[it, k], rs.at[it, k], rr.at[it, k], row_peer(k))
            copy.start()
            pending.append(copy)

    def take_rows(it, dest):
        total = rowb[it, 0]
        for k in range(1, group):
            remote(rowb.at[it, 0], rowb.at[it, k], rs.at[it, k], rr.at[it, k], row_peer(k)).wait_recv()
            total = total + rowb[it, k]
        inv = 1.0 / total
        for i in range(images // 128):
            dest[i * 128:(i + 1) * 128, :] = jnp.broadcast_to(inv[i:i + 1, :], (128, 128)).T

    def row_pass(it):
        def body(rb, _):
            rows = aligned(rb * 128, 128)
            acc = expo[rows, 0:128] * psb[:, 0:128]
            for i in range(1, protos // 128):
                acc += expo[rows, i * 128:(i + 1) * 128] * psb[:, i * 128:(i + 1) * 128]
            rowb[it, 0, pl.ds(rb, 1), :] = jnp.sum(acc.T, axis=0, keepdims=True)
            return 0
        lax.fori_loop(0, images // 128, body, 0)

    def col_pass():
        cacc[...] = jnp.zeros_like(cacc)

        def body(rb, _):
            rows = aligned(rb * 128, 128)
            scale = rscale[rows, :]
            for i in range(protos // 128):
                part = expo[rows, i * 128:(i + 1) * 128] * scale
                cacc[:, i * 128:(i + 1) * 128] += jnp.sum(part.reshape(16, 8, 128), axis=0)
            return 0
        lax.fori_loop(0, images // 128, body, 0)

    teacher_block(o)
    gather_forward(0, tdir)
    for k in range(1, OUTER):
        gather_wait(0, tdir, k)
        teacher_block(from_z(k))
    send_cols(0)
    load_s.wait()
    normalize(sw)
    gather_forward(1, sdir)
    student_block(o)
    fill = 1
    for it in range(ITERS):
        if it > 0:
            col_pass()
            send_cols(it)
            if fill < OUTER:
                gather_wait(1, sdir, fill)
                student_block(from_z(fill))
                fill += 1
                if fill == OUTER:
                    send_rows(ITERS)
            else:
                take_rows(ITERS, tscale)
        take_cols(it)
        row_pass(it)
        send_rows(it)
        if fill < OUTER:
            gather_wait(1, sdir, fill)
            student_block(from_z(fill))
            fill += 1
            if fill == OUTER:
                send_rows(ITERS)
        take_rows(it, rscale)

    def final_chunk(start):
        cols = aligned(start, width)

        def tile(ib, _):
            rows = aligned(ib * block, block)
            es = jnp.exp2(dot(sdir[rows, :], sw[cols, :], (1, 1)) * ks)
            it_, r_ = tscale[rows, :], rscale[rows, :]
            for i in range(width // 128):
                sub = aligned(start + i * 128, 128)
                tgt = expo[rows, sub] * psb[:, sub] * r_
                df = es[:, i * 128:(i + 1) * 128] * it_ - tgt
                diffs[rows, i * 128:(i + 1) * 128] = df.astype(bf16)
            feat[rows, :] += dot(diffs[rows, :], sw[cols, :], (1, 0))
            return 0
        lax.fori_loop(0, OUTER, tile, 0)
        gw_t = dot(sdir_t[...], diffs[...], (1, 0))
        gws[cols, :] = gw_t.T.astype(bf16)

    def gw_copy(k):
        target = lax.rem(q + k, inner)
        return remote(
            gws.at[aligned(target * rows_out, rows_out)], gwr.at[k], ws.at[k], wr.at[k],
            (o * inner + target, c),
        )

    feat[...] = jnp.zeros_like(feat)
    if rows_out % width == 0:
        def per_block(k, _):
            first = lax.rem(q + k, inner) * rows_out

            def inside(s, _):
                final_chunk(first + s * width)
                return 0
            lax.fori_loop(0, rows_out // width, inside, 0)

            @pl.when(k < inner)
            def _():
                gw_copy(k).start()
            return 0
        lax.fori_loop(1, inner + 1, per_block, 0)
    else:
        def per_chunk(n, _):
            final_chunk(n * width)
            return 0
        lax.fori_loop(0, chunks, per_chunk, 0)
        for k in range(1, inner):
            gw_copy(k).start()

    for j in range(1, cores):
        other = lax.rem(c + j, cores)
        for ob in range(OUTER):
            fxs[j, ob * strip:(ob + 1) * strip, :] = feat[aligned(ob * block + other * strip, strip), :].astype(bf16)
        copy = remote(fxs.at[j], fxr.at[j], xs.at[j], xr.at[j], core_peer(j))
        copy.start()
        pending.append(copy)
    for j in range(1, cores):
        remote(fxs.at[j], fxr.at[j], xs.at[j], xr.at[j], core_peer(j)).wait_recv()

    def strip_sum(ob):
        total = feat[aligned(ob * block + c * strip, strip), :]
        for j in range(1, cores):
            total = total + fxr[j, aligned(ob * strip, strip), :].astype(f32)
        return total

    for k in range(1, OUTER):
        fzs[k] = strip_sum(lax.rem(o + k, OUTER)).astype(bf16)
        copy = remote(fzs.at[k], fzr.at[k], zs.at[k], zr.at[k], z_peer(k))
        copy.start()
        pending.append(copy)

    for k in range(1, inner):
        gw_copy(k).wait_recv()
    scale_p = protos_all / (student_temp * math.sqrt(images_all))
    step = min(256, rows_out)

    def proto_rows(n, _):
        rows = aligned(n * step, step)
        gw = gws[aligned(q * rows_out + n * step, step), :].astype(f32)
        for k in range(1, inner):
            gw = gw + gwr[k, rows, :].astype(f32)
        gw = gw * scale_p
        v = vown[rows, :].astype(f32)
        rt = factor_of(v)
        out_p[rows, :] = rt * gw - v * (rt * rt * rt) * jnp.sum(v * gw, axis=-1, keepdims=True)
        return 0
    load_v.wait()
    lax.fori_loop(0, rows_out // step, proto_rows, 0)

    total = strip_sum(o)
    for k in range(1, OUTER):
        remote(fzs.at[k], fzr.at[k], zs.at[k], zr.at[k], z_peer(k)).wait_recv()
        total = total + fzr[k].astype(f32)
    gz = total * (math.sqrt(protos_all) / student_temp)
    mine = aligned(c * strip, strip)
    z = sf[mine, :].astype(f32)
    rt = factor_of(z)
    fo[mine, :] = rt * gz - z * (rt * rt * rt) * jnp.sum(z * gz, axis=-1, keepdims=True)
    for j in range(1, cores):
        part = fo.at[mine]
        copy = remote(part, part, os_.at[j], or_.at[j], core_peer(j))
        copy.start()
        pending.append(copy)
    for j in range(1, cores):
        part = fo.at[aligned(from_core(j) * strip, strip)]
        remote(part, part, os_.at[j], or_.at[j], core_peer(j)).wait_recv()
    out_f[...] = fo[...]
    for k in range(1, inner):
        gw_copy(k).wait_send()
    for copy in pending:
        copy.wait_send()


def shards(teacher_feats, student_feats, teacher_protos, student_protos):
    block, bot = teacher_feats.shape
    proto_local = teacher_protos.shape[0]
    dp, cores = lax.axis_size("dp"), lax.axis_size("proto")
    inner = dp // OUTER
    group = OUTER * cores
    images, protos = block * OUTER, proto_local // OUTER
    rows_out = proto_local // dp
    strip = block // cores
    width = min(512, protos)
    vmem, dma = pltpu.VMEM, pltpu.SemaphoreType.DMA
    scratch = [
        vmem((images, protos), f32),
        vmem((protos, bot), bf16),
        vmem((protos, bot), bf16),
        vmem((rows_out, bot), bf16),
        vmem((images, bot), bf16),
        vmem((images, bot), bf16),
        vmem((bot, images), bf16),
        vmem((images, 128), f32),
        vmem((images, 128), f32),
        vmem((8, protos), f32),
        vmem((block, 128), f32),
        vmem((images, width), bf16),
        vmem((protos, bot), bf16),
        vmem((inner, rows_out, bot), bf16),
        vmem((images, bot), f32),
        vmem((cores, OUTER * strip, bot), bf16),
        vmem((cores, OUTER * strip, bot), bf16),
        vmem((OUTER, strip, bot), bf16),
        vmem((OUTER, strip, bot), bf16),
        vmem((block, bot), f32),
        vmem((ITERS, inner, 1, protos), f32),
        vmem((1, protos), f32),
        vmem((ITERS + 1, group, images // 128, 128), f32),
        dma((3,)),
        dma((2, OUTER)), dma((2, OUTER)),
        dma((2, OUTER, cores)), dma((2, OUTER, cores)),
        dma((ITERS, inner)), dma((ITERS, inner)),
        dma((ITERS + 1, group)), dma((ITERS + 1, group)),
        dma((inner,)), dma((inner,)),
        dma((cores,)), dma((cores,)),
        dma((OUTER,)), dma((OUTER,)),
        dma((cores,)), dma((cores,)),
    ]
    whole = pl.BlockSpec(memory_space=pltpu.VMEM)
    return pl.pallas_call(
        functools.partial(kernel, inner, cores, proto_local * cores, block * dp),
        out_shape=(
            jax.ShapeDtypeStruct((rows_out, bot), f32),
            jax.ShapeDtypeStruct((block, bot), f32),
        ),
        in_specs=[whole, whole, pl.BlockSpec(memory_space=pl.ANY), pl.BlockSpec(memory_space=pl.ANY)],
        out_specs=(whole, whole),
        scratch_shapes=scratch,
        compiler_params=pltpu.CompilerParams(
            collective_id=0, has_side_effects=True, vmem_limit_bytes=63 * 1024 * 1024
        ),
    )(teacher_feats, student_feats, teacher_protos, student_protos)


def solution(mesh):
    in_specs = (P("dp", None), P("dp", None), P("proto", None), P("proto", None))
    out_specs = (P(("proto", "dp"), None), P("dp", None))
    return jax.shard_map(shards, mesh=mesh, in_specs=in_specs, out_specs=out_specs, check_vma=False)
```

```python
import functools
import math

import jax
import jax.numpy as jnp
from jax import lax
from jax.experimental import pallas as pl
from jax.experimental.pallas import tpu as pltpu
from jax.sharding import PartitionSpec as P

ITERS = 3
OUTER = 4

teacher_temp = 0.07
student_temp = 0.1
norm_eps = 1e-06
LOG2E = math.log2(math.e)
MESH = pl.DeviceIdType.MESH
f32 = jnp.float32
bf16 = jnp.bfloat16


def dot(a, b, dims):
    return lax.dot_general(a, b, ((dims[:1], dims[1:]), ((), ())), preferred_element_type=f32)


def factor_of(wide):
    return lax.rsqrt(jnp.sum(wide * wide, axis=-1, keepdims=True) + norm_eps)


def unit(value):
    wide = value.astype(f32)
    return (wide * factor_of(wide)).astype(bf16)


def kernel(
    inner, cores, protos_all, images_all,
    tf, sf, tp, sp, out_p, out_f,
    expo, tw, sw, vown, tdir, sdir, sdir_t, rscale, tscale, cacc, tacc, diffs,
    gws, gwr, feat, fxs, fxr, fzs, fzr, fo, colb, psb, rowb,
    lsem, g1s, g1r, g2s, g2r, cs, cr, rs, rr, ws, wr, xs, xr, zs, zr, os_, or_,
):
    block = tf.shape[0]
    strip = block // cores
    images, protos = expo.shape
    rows_out = out_p.shape[0]
    width = min(512, protos)
    chunks = protos // width
    group = OUTER * cores
    d, c = lax.axis_index("dp"), lax.axis_index("proto")
    o, q = d // inner, lax.rem(d, inner)
    g = o * cores + c
    kt, ks = LOG2E / teacher_temp, LOG2E / student_temp

    def col_peer(k):
        return (o * inner + lax.rem(q + k, inner), c)

    def row_peer(k):
        h = lax.rem(g + k, group)
        return ((h // cores) * inner + q, lax.rem(h, cores))

    def z_peer(k):
        return (lax.rem(o + k, OUTER) * inner + q, c)

    def core_peer(j):
        return (d, lax.rem(c + j, cores))

    def from_z(k):
        return lax.rem(o + OUTER - k, OUTER)

    def from_core(j):
        return lax.rem(c + cores - j, cores)

    def aligned(start, size):
        return pl.ds(pl.multiple_of(start, size), size)

    def remote(src, dst, ss, rsm, dev):
        return pltpu.make_async_remote_copy(
            src_ref=src, dst_ref=dst, send_sem=ss, recv_sem=rsm,
            device_id=dev, device_id_type=MESH,
        )

    load_t = pltpu.make_async_copy(tp.at[aligned(o * protos, protos)], tw, lsem.at[0])
    load_s = pltpu.make_async_copy(sp.at[aligned(o * protos, protos)], sw, lsem.at[1])
    load_v = pltpu.make_async_copy(sp.at[aligned(d * rows_out, rows_out)], vown, lsem.at[2])
    load_t.start()
    load_s.start()
    load_v.start()

    barrier = pltpu.get_barrier_semaphore()
    for k in range(1, inner):
        pl.semaphore_signal(barrier, inc=1, device_id=col_peer(k), device_id_type=MESH)
    for k in range(1, group):
        pl.semaphore_signal(barrier, inc=1, device_id=row_peer(k), device_id_type=MESH)
    own = aligned(o * block, block)
    tdir[own, :] = unit(tf[...])
    sdir[own, :] = unit(sf[...])
    pl.semaphore_wait(barrier, inner - 1 + group - 1)

    pending = []

    def strip_rows(buf, ob, part):
        return buf.at[aligned(ob * block + part * strip, strip)]

    def gather_first(n, buf):
        for k in range(1, OUTER):
            part = strip_rows(buf, o, c)
            copy = remote(part, part, g1s.at[n, k], g1r.at[n, k], z_peer(k))
            copy.start()
            pending.append(copy)

    def gather_forward(n, buf):
        for k in range(1, OUTER):
            part = strip_rows(buf, from_z(k), c)
            remote(part, part, g1s.at[n, k], g1r.at[n, k], z_peer(k)).wait_recv()
            for j in range(1, cores):
                copy = remote(part, part, g2s.at[n, k, j], g2r.at[n, k, j], core_peer(j))
                copy.start()
                pending.append(copy)

    def gather_wait(n, buf, k):
        for j in range(1, cores):
            part = strip_rows(buf, from_z(k), from_core(j))
            remote(part, part, g2s.at[n, k, j], g2r.at[n, k, j], core_peer(j)).wait_recv()

    gather_first(0, tdir)

    def normalize(buf):
        def body(n, _):
            rows = aligned(n * width, width)
            buf[rows, :] = unit(buf[rows, :])
            return 0
        lax.fori_loop(0, chunks, body, 0)

    load_t.wait()
    normalize(tw)

    cacc[...] = jnp.zeros_like(cacc)

    def teacher_block(ob):
        rows = aligned(ob * block, block)

        def body(n, _):
            cols = aligned(n * width, width)
            e = jnp.exp2(dot(tdir[rows, :], tw[cols, :], (1, 1)) * kt)
            expo[rows, cols] = e
            cacc[:, cols] += jnp.sum(e.reshape(block // 8, 8, width), axis=0)
            return 0
        lax.fori_loop(0, chunks, body, 0)

    def student_block(ob):
        rows = aligned(ob * block, block)
        tacc[...] = jnp.zeros_like(tacc)

        def body(n, _):
            cols = aligned(n * width, width)
            e = jnp.exp2(dot(sdir[rows, :], sw[cols, :], (1, 1)) * ks)
            part = e[:, :128]
            for i in range(1, width // 128):
                part += e[:, i * 128:(i + 1) * 128]
            tacc[...] += part
            return 0
        lax.fori_loop(0, chunks, body, 0)
        for i in range(block // 128):
            line = jnp.sum(tacc[i * 128:(i + 1) * 128, :].T, axis=0, keepdims=True)
            rowb[ITERS, 0, pl.ds(ob * (block // 128) + i, 1), :] = line
        sdir_t[:, rows] = sdir[rows, :].T

    def send_cols(it):
        colb[it, 0] = jnp.sum(cacc[...], axis=0, keepdims=True)
        for k in range(1, inner):
            copy = remote(colb.at[it, 0], colb.at[it, k], cs.at[it, k], cr.at[it, k], col_peer(k))
            copy.start()
            pending.append(copy)

    def take_cols(it):
        total = colb[it, 0]
        for k in range(1, inner):
            remote(colb.at[it, 0], colb.at[it, k], cs.at[it, k], cr.at[it, k], col_peer(k)).wait_recv()
            total = total + colb[it, k]
        psb[...] = 1.0 / total

    def send_rows(it):
        for k in range(1, group):
            copy = remote(rowb.at[it, 0], rowb.at[it, k], rs.at[it, k], rr.at[it, k], row_peer(k))
            copy.start()
            pending.append(copy)

    def take_rows(it, dest):
        total = rowb[it, 0]
        for k in range(1, group):
            remote(rowb.at[it, 0], rowb.at[it, k], rs.at[it, k], rr.at[it, k], row_peer(k)).wait_recv()
            total = total + rowb[it, k]
        inv = 1.0 / total
        for i in range(images // 128):
            dest[i * 128:(i + 1) * 128, :] = jnp.broadcast_to(inv[i:i + 1, :], (128, 128)).T

    def row_pass(it):
        def body(rb, _):
            rows = aligned(rb * 128, 128)
            acc = expo[rows, 0:128] * psb[:, 0:128]
            for i in range(1, protos // 128):
                acc += expo[rows, i * 128:(i + 1) * 128] * psb[:, i * 128:(i + 1) * 128]
            rowb[it, 0, pl.ds(rb, 1), :] = jnp.sum(acc.T, axis=0, keepdims=True)
            return 0
        lax.fori_loop(0, images // 128, body, 0)

    def col_pass():
        cacc[...] = jnp.zeros_like(cacc)

        def body(rb, _):
            rows = aligned(rb * 128, 128)
            scale = rscale[rows, :]
            for i in range(protos // 128):
                part = expo[rows, i * 128:(i + 1) * 128] * scale
                cacc[:, i * 128:(i + 1) * 128] += jnp.sum(part.reshape(16, 8, 128), axis=0)
            return 0
        lax.fori_loop(0, images // 128, body, 0)

    teacher_block(o)
    gather_forward(0, tdir)
    gather_first(1, sdir)
    for k in range(1, OUTER):
        gather_wait(0, tdir, k)
        teacher_block(from_z(k))
    send_cols(0)
    load_s.wait()
    normalize(sw)
    gather_forward(1, sdir)
    student_block(o)
    fill = 1
    for it in range(ITERS):
        if it > 0:
            col_pass()
            send_cols(it)
            if fill < OUTER:
                gather_wait(1, sdir, fill)
                student_block(from_z(fill))
                fill += 1
                if fill == OUTER:
                    send_rows(ITERS)
            else:
                take_rows(ITERS, tscale)
        take_cols(it)
        row_pass(it)
        send_rows(it)
        if fill < OUTER:
            gather_wait(1, sdir, fill)
            student_block(from_z(fill))
            fill += 1
            if fill == OUTER:
                send_rows(ITERS)
        take_rows(it, rscale)

    def final_chunk(start):
        cols = aligned(start, width)

        def tile(ib, _):
            rows = aligned(ib * block, block)
            es = jnp.exp2(dot(sdir[rows, :], sw[cols, :], (1, 1)) * ks)
            it_, r_ = tscale[rows, :], rscale[rows, :]
            for i in range(width // 128):
                sub = aligned(start + i * 128, 128)
                tgt = expo[rows, sub] * psb[:, sub] * r_
                df = es[:, i * 128:(i + 1) * 128] * it_ - tgt
                diffs[rows, i * 128:(i + 1) * 128] = df.astype(bf16)
            feat[rows, :] += dot(diffs[rows, :], sw[cols, :], (1, 0))
            return 0
        lax.fori_loop(0, OUTER, tile, 0)
        gw_t = dot(sdir_t[...], diffs[...], (1, 0))
        gws[cols, :] = gw_t.T.astype(bf16)

    pieces = rows_out // width if rows_out % width == 0 else 1
    piece = rows_out // pieces

    def gw_copy(k, s):
        target = lax.rem(q + k, inner)
        return remote(
            gws.at[aligned(target * rows_out + s * piece, piece)],
            gwr.at[k, aligned(s * piece, piece)], ws.at[k, s], wr.at[k, s],
            (o * inner + target, c),
        )

    feat[...] = jnp.zeros_like(feat)
    if rows_out % width == 0:
        def per_block(k, _):
            first = lax.rem(q + k, inner) * rows_out

            def inside(s, _):
                final_chunk(first + s * width)

                @pl.when(k < inner)
                def _():
                    gw_copy(k, s).start()
                return 0
            lax.fori_loop(0, pieces, inside, 0)
            return 0
        lax.fori_loop(1, inner + 1, per_block, 0)
    else:
        def per_chunk(n, _):
            final_chunk(n * width)
            return 0
        lax.fori_loop(0, chunks, per_chunk, 0)
        for k in range(1, inner):
            gw_copy(k, 0).start()

    def fx_copy(j, k):
        part = pl.ds(k * strip, strip)
        return remote(fxs.at[j, part], fxr.at[j, part], xs.at[j, k], xr.at[j, k], core_peer(j))

    order = [*range(1, OUTER), 0]
    for k in order:
        ob = lax.rem(o + k, OUTER)
        for j in range(1, cores):
            other = lax.rem(c + j, cores)
            fxs[j, k * strip:(k + 1) * strip, :] = feat[aligned(ob * block + other * strip, strip), :].astype(bf16)
            copy = fx_copy(j, k)
            copy.start()
            pending.append(copy)

    def strip_sum(k):
        ob = lax.rem(o + k, OUTER)
        total = feat[aligned(ob * block + c * strip, strip), :]
        for j in range(1, cores):
            fx_copy(j, k).wait_recv()
            total = total + fxr[j, k * strip:(k + 1) * strip, :].astype(f32)
        return total

    for k in range(1, OUTER):
        fzs[k] = strip_sum(k).astype(bf16)
        copy = remote(fzs.at[k], fzr.at[k], zs.at[k], zr.at[k], z_peer(k))
        copy.start()
        pending.append(copy)

    for k in range(1, inner):
        for s in range(pieces):
            gw_copy(k, s).wait_recv()
    scale_p = protos_all / (student_temp * math.sqrt(images_all))
    step = min(256, rows_out)

    def proto_rows(n, _):
        rows = aligned(n * step, step)
        gw = gws[aligned(q * rows_out + n * step, step), :].astype(f32)
        for k in range(1, inner):
            gw = gw + gwr[k, rows, :].astype(f32)
        gw = gw * scale_p
        v = vown[rows, :].astype(f32)
        rt = factor_of(v)
        out_p[rows, :] = rt * gw - v * (rt * rt * rt) * jnp.sum(v * gw, axis=-1, keepdims=True)
        return 0
    load_v.wait()
    lax.fori_loop(0, rows_out // step, proto_rows, 0)

    total = strip_sum(0)
    for k in range(1, OUTER):
        remote(fzs.at[k], fzr.at[k], zs.at[k], zr.at[k], z_peer(k)).wait_recv()
        total = total + fzr[k].astype(f32)
    gz = total * (math.sqrt(protos_all) / student_temp)
    mine = aligned(c * strip, strip)
    z = sf[mine, :].astype(f32)
    rt = factor_of(z)
    fo[mine, :] = rt * gz - z * (rt * rt * rt) * jnp.sum(z * gz, axis=-1, keepdims=True)
    for j in range(1, cores):
        part = fo.at[mine]
        copy = remote(part, part, os_.at[j], or_.at[j], core_peer(j))
        copy.start()
        pending.append(copy)
    for j in range(1, cores):
        part = fo.at[aligned(from_core(j) * strip, strip)]
        remote(part, part, os_.at[j], or_.at[j], core_peer(j)).wait_recv()
    out_f[...] = fo[...]
    for k in range(1, inner):
        for s in range(pieces):
            gw_copy(k, s).wait_send()
    for copy in pending:
        copy.wait_send()


def shards(teacher_feats, student_feats, teacher_protos, student_protos):
    block, bot = teacher_feats.shape
    proto_local = teacher_protos.shape[0]
    dp, cores = lax.axis_size("dp"), lax.axis_size("proto")
    inner = dp // OUTER
    group = OUTER * cores
    images, protos = block * OUTER, proto_local // OUTER
    rows_out = proto_local // dp
    strip = block // cores
    width = min(512, protos)
    pieces = rows_out // width if rows_out % width == 0 else 1
    vmem, dma = pltpu.VMEM, pltpu.SemaphoreType.DMA
    scratch = [
        vmem((images, protos), f32),
        vmem((protos, bot), bf16),
        vmem((protos, bot), bf16),
        vmem((rows_out, bot), bf16),
        vmem((images, bot), bf16),
        vmem((images, bot), bf16),
        vmem((bot, images), bf16),
        vmem((images, 128), f32),
        vmem((images, 128), f32),
        vmem((8, protos), f32),
        vmem((block, 128), f32),
        vmem((images, width), bf16),
        vmem((protos, bot), bf16),
        vmem((inner, rows_out, bot), bf16),
        vmem((images, bot), f32),
        vmem((cores, OUTER * strip, bot), bf16),
        vmem((cores, OUTER * strip, bot), bf16),
        vmem((OUTER, strip, bot), bf16),
        vmem((OUTER, strip, bot), bf16),
        vmem((block, bot), f32),
        vmem((ITERS, inner, 1, protos), f32),
        vmem((1, protos), f32),
        vmem((ITERS + 1, group, images // 128, 128), f32),
        dma((3,)),
        dma((2, OUTER)), dma((2, OUTER)),
        dma((2, OUTER, cores)), dma((2, OUTER, cores)),
        dma((ITERS, inner)), dma((ITERS, inner)),
        dma((ITERS + 1, group)), dma((ITERS + 1, group)),
        dma((inner, pieces)), dma((inner, pieces)),
        dma((cores, OUTER)), dma((cores, OUTER)),
        dma((OUTER,)), dma((OUTER,)),
        dma((cores,)), dma((cores,)),
    ]
    whole = pl.BlockSpec(memory_space=pltpu.VMEM)
    return pl.pallas_call(
        functools.partial(kernel, inner, cores, proto_local * cores, block * dp),
        out_shape=(
            jax.ShapeDtypeStruct((rows_out, bot), f32),
            jax.ShapeDtypeStruct((block, bot), f32),
        ),
        in_specs=[whole, whole, pl.BlockSpec(memory_space=pl.ANY), pl.BlockSpec(memory_space=pl.ANY)],
        out_specs=(whole, whole),
        scratch_shapes=scratch,
        compiler_params=pltpu.CompilerParams(
            collective_id=0, has_side_effects=True, vmem_limit_bytes=63 * 1024 * 1024
        ),
    )(teacher_feats, student_feats, teacher_protos, student_protos)


def solution(mesh):
    in_specs = (P("dp", None), P("dp", None), P("proto", None), P("proto", None))
    out_specs = (P(("proto", "dp"), None), P("dp", None))
    return jax.shard_map(shards, mesh=mesh, in_specs=in_specs, out_specs=out_specs, check_vma=False)
```
